32 devices in a mesh: replica: 8 (over y, x, core), shard: 4 (over z).
Axes of the slice: x: 2, y: 2, z: 4, core: 2. Of those that a mesh axis runs over, the one named last changes fastest.
Arguments:
- features: bfloat16 [8192, 8192], P(('replica', 'shard')), may hold values from -6 to 6
- key_grads: bfloat16 [8192, 1024], P(('replica', 'shard')), may hold values from -1.5 to 1.5
- key_weight: bfloat16 [8192, 1024], P('shard'), may hold values from -0.1875 to 0.1875
- momentum: float32 [8, 8192, 1024], P('replica', 'shard'), may hold values from -8 to 8
- worker_error: float32 [8, 8192, 1024], P('replica', 'shard'), may hold values from -2 to 2
- server_error: float32 [4, 2048, 1024], P('shard', 'replica'), may hold values from -2 to 2
Outputs:
- input_grads: bfloat16 [8192, 8192], P(('replica', 'shard'))
- synced_momentum: bfloat16 [8192, 1024], P('shard')
- new_worker_error: float32 [8, 8192, 1024], P('replica', 'shard')
- new_server_error: float32 [4, 2048, 1024], P('shard', 'replica')
The draws below stay inside these ranges and needn't reach their ends.
All inputs are finite; a program needn't handle non-finite values. Where the reference program divides by a largest or mean magnitude, that divisor is 1e-20 or more.
Results may differ from the reference program's by a relative error of at most 0.018.
Values may be sent and summed in bfloat16 or wider, within the bound.
A program may use at most 128 MiB of HBM per device.

```python
import jax
import jax.numpy as jnp
from jax import lax

D = 8192
KVD = 1024
TOK_DEV = 256
REPLICAS = 8
ROWS = 8192
SHARD_ROWS = 2048
N_SHARD = 4


def draw_momentum(key, part):
    key_rows, key_cols, key_base = jax.random.split(key, 3)
    row_scale = jnp.exp(jax.random.uniform(key_rows, (REPLICAS, D, 1), minval=-1.2, maxval=1.2))
    col_scale = jnp.exp(jax.random.uniform(key_cols, (1, 1, KVD), minval=-0.6, maxval=0.6))
    base = jax.random.normal(key_base, (REPLICAS, D, KVD), dtype=jnp.float32)
    return jnp.clip(0.5 * base * row_scale * col_scale, -8.0, 8.0).astype(jnp.float32)


def spiked(array, stream_key, source, target, blocks, factor):
    def block_of(axis_at):
        return (jnp.arange(array.shape[axis_at]) // (array.shape[axis_at] // blocks)).reshape((-1,) + (1,) * (array.ndim - 1 - axis_at))

    one_side = jax.random.permutation(stream_key, blocks)[block_of(target)]
    other_side = (block_of(target) + blocks // 2) % blocks
    return jnp.where((block_of(source) == one_side) | (block_of(source) == other_side), factor * array, array)


def block_levels(key, dims, shards, low, high):
    level, own = 1.0, jax.random.fold_in(key, 6)
    for position, parts in shards:
        heights = jnp.exp(jax.random.uniform(jax.random.fold_in(own, position), (parts,), jnp.float32, low / len(shards), high / len(shards)))
        level = level * jnp.repeat(heights, dims[position] // parts).reshape([-1 if axis == position else 1 for axis in range(len(dims))])
    return level


def noise(stream_key, extent, deviation, reach, shards=(), kind=jnp.bfloat16):
    loudness = block_levels(stream_key, extent, shards, -0.22, 0.18) if shards else 1.0
    drawn = jax.random.normal(stream_key, extent, jnp.float32) * deviation * loudness
    return jnp.minimum(jnp.maximum(drawn, -reach), reach).astype(kind)


def heavy_noise(own_key, extent, spread, limit, cuts, heavy, held_as=jnp.bfloat16):
    result = spread * jax.random.normal(own_key, extent, jnp.float32)
    if cuts:
        result = result * block_levels(own_key, extent, cuts, -0.22, 0.18)
    return jnp.clip(spiked(result, jax.random.fold_in(own_key, 3), *heavy), -limit, limit).astype(held_as)


def setup_inputs(seed: int = 0) -> dict:
    keys = jax.random.split(jax.random.key(seed), 7)
    features = heavy_noise(keys[0], (ROWS, D), 1.0, 6.0, ((0, 32),), (0, 1, 32, 2.75))
    key_grads = noise(keys[1], (ROWS, KVD), 0.25, 1.5, ((0, 32),))
    key_weight = noise(keys[2], (D, KVD), KVD ** -0.5, 0.1875, ((0, 4),))
    momentum = draw_momentum(jax.random.fold_in(keys[6], 71), 0)
    worker_error = noise(keys[4], (REPLICAS, D, KVD), 0.3, 2.0, ((0, 8), (1, 4)), jnp.float32)
    server_error = noise(keys[5], (N_SHARD, SHARD_ROWS, KVD), 0.3, 2.0, ((0, 4), (1, 8)), jnp.float32)
    return dict(features=features, key_grads=key_grads, key_weight=key_weight, momentum=momentum, worker_error=worker_error, server_error=server_error)


decay_rate = 0.9


def compress(values):
    scale = jnp.mean(jnp.abs(values), axis=-1, keepdims=True) + 1e-6
    return (scale * jnp.tanh(values / scale)).astype(jnp.bfloat16)


def reference(features, key_grads, key_weight, momentum, worker_error, server_error):
    blocks = features.reshape(REPLICAS, N_SHARD, TOK_DEV, D)
    grad_blocks = key_grads.reshape(REPLICAS, N_SHARD, TOK_DEV, KVD)

    def replica_step(items):
        inputs, grads, moment, error = items

        def add_part(total, pair):
            part = jnp.dot(pair[0].T, pair[1], preferred_element_type=jnp.float32).astype(jnp.bfloat16)
            part = lax.optimization_barrier(part)
            return total + part.astype(jnp.float32), None

        weight_grad, _ = lax.scan(add_part, jnp.zeros((D, KVD), jnp.float32), (inputs, grads))
        flat = grads.reshape(N_SHARD * TOK_DEV, KVD)
        back = jnp.dot(flat, key_weight.T, preferred_element_type=jnp.float32).astype(jnp.bfloat16)
        value = decay_rate * moment + (1.0 - decay_rate) * weight_grad + error
        packed = compress(value)
        return back, value - packed.astype(jnp.float32), packed

    back, new_worker, packed = lax.map(replica_step, (blocks, grad_blocks, momentum, worker_error))
    held = jnp.sum(packed.astype(jnp.float32), axis=0) / REPLICAS + server_error.reshape(D, KVD)
    synced = compress(held)
    new_server = (held - synced.astype(jnp.float32)).reshape(N_SHARD, SHARD_ROWS, KVD)
    return back.reshape(ROWS, D), synced, new_worker, new_server
```

```python
import functools

import jax
import jax.numpy as jnp
from jax import lax
from jax.experimental import pallas as pl
from jax.experimental.pallas import tpu as pltpu
from jax.sharding import PartitionSpec as P

decay_rate = 0.9


def compress(values):
    scale = jnp.mean(jnp.abs(values), axis=-1, keepdims=True) + 1e-06
    return (scale * jnp.tanh(values / scale)).astype(jnp.bfloat16)


def worker_kernel(cols_ref, grads_ref, moment_ref, error_ref, new_ref, packed_ref):
    grad = lax.dot_general(
        cols_ref[...], grads_ref[...], (((0,), (0,)), ((), ())), preferred_element_type=jnp.float32
    )
    value = decay_rate * moment_ref[0] + (1.0 - decay_rate) * grad + error_ref[0]
    packed = compress(value)
    new_ref[0] = value - packed.astype(jnp.float32)
    packed_ref[...] = packed


def worker_step(columns, all_grads, momentum, worker_error):
    tokens, rows = columns.shape
    width = all_grads.shape[1]
    chunk = min(256, rows)
    block = pl.BlockSpec((1, chunk, width), lambda i: (0, i, 0))
    return pl.pallas_call(
        worker_kernel,
        grid=(rows // chunk,),
        in_specs=[
            pl.BlockSpec((tokens, chunk), lambda i: (0, i)),
            pl.BlockSpec((tokens, width), lambda i: (0, 0)),
            block,
            block,
        ],
        out_specs=[block, pl.BlockSpec((chunk, width), lambda i: (i, 0))],
        out_shape=[
            jax.ShapeDtypeStruct(momentum.shape, jnp.float32),
            jax.ShapeDtypeStruct((rows, width), jnp.bfloat16),
        ],
        compiler_params=pltpu.CompilerParams(vmem_limit_bytes=40 * 2**20),
        cost_estimate=pl.CostEstimate(
            flops=2 * tokens * rows * width,
            bytes_accessed=14 * rows * width + 2 * tokens * (rows + width),
            transcendentals=rows * width,
        ),
    )(columns, all_grads, momentum, worker_error)


def per_device(features, key_grads, key_weight, momentum, worker_error, server_error):
    replica_count = lax.axis_size("replica")
    kv_width = key_weight.shape[1]
    share = key_weight.shape[0] // replica_count
    mine = lax.dynamic_slice_in_dim(key_weight, lax.axis_index("replica") * share, share, 0)
    all_grads = lax.all_gather(key_grads, "shard", axis=0, tiled=True)
    columns = lax.all_to_all(features, "shard", split_axis=1, concat_axis=0, tiled=True)
    all_weight = lax.all_gather(mine, ("shard", "replica"), axis=0, tiled=True)
    new_worker, packed = worker_step(columns, all_grads, momentum, worker_error)
    received = lax.all_to_all(packed, "replica", split_axis=0, concat_axis=0, tiled=True)
    owned_rows = server_error.shape[1]
    stacked = received.reshape(replica_count, owned_rows, kv_width).astype(jnp.float32)
    held = jnp.sum(stacked, axis=0) / replica_count + server_error[0]
    synced_block = compress(held)
    new_server = (held - synced_block.astype(jnp.float32))[None]
    synced = lax.all_gather(synced_block, "replica", axis=0, tiled=True)
    input_grads = lax.dot_general(
        key_grads, all_weight, (((1,), (1,)), ((), ())), preferred_element_type=jnp.float32
    ).astype(jnp.bfloat16)
    return (input_grads, synced, new_worker, new_server)


def solution(mesh):
    in_specs = (
        P(("replica", "shard"), None),
        P(("replica", "shard"), None),
        P("shard", None),
        P("replica", "shard", None),
        P("replica", "shard", None),
        P("shard", "replica", None),
    )
    out_specs = (
        P(("replica", "shard"), None),
        P("shard", None),
        P("replica", "shard", None),
        P("shard", "replica", None),
    )
    return jax.shard_map(
        per_device, mesh=mesh, in_specs=in_specs, out_specs=out_specs, check_vma=False
    )
```

```python
import functools

import jax
import jax.numpy as jnp
from jax import lax
from jax.experimental import pallas as pl
from jax.experimental.pallas import tpu as pltpu
from jax.sharding import PartitionSpec as P

MESH = pl.DeviceIdType.MESH

decay_rate = 0.9


def compress(values):
    scale = jnp.mean(jnp.abs(values), axis=-1, keepdims=True) + 1e-06
    return (scale * jnp.tanh(values / scale)).astype(jnp.bfloat16)


def exchange_kernel(
    shards, replicas, features, grads, weight, moment, error, server,
    input_grads, synced, new_worker, new_server,
    block, held_weight, back, cols, all_grads, mom, err, packed, got, total,
    grad_local, grad_send, grad_recv, load, col_send, col_recv, store, pack_send, pack_recv,
    weight_load, back_local, back_send, back_recv, sync_local, sync_send, sync_recv,
):
    r, s = lax.axis_index("replica"), lax.axis_index("shard")
    tokens = grads.shape[0]
    chunks, rows = mom.shape[0], mom.shape[1]
    owned = got.shape[1]
    per = rows // owned
    shard_rows = chunks * rows
    first = r // per + 1

    barrier = pltpu.get_barrier_semaphore()
    for d in range(1, shards):
        pl.semaphore_signal(barrier, inc=1, device_id=(r, lax.rem(s + d, shards)), device_id_type=MESH)
    for d in range(1, replicas):
        pl.semaphore_signal(barrier, inc=1, device_id=(lax.rem(r + d, replicas), s), device_id_type=MESH)
    pl.semaphore_wait(barrier, shards + replicas - 2)

    def grad_copy(d):
        return pltpu.make_async_remote_copy(
            src_ref=grads,
            dst_ref=all_grads.at[pl.ds(d * tokens, tokens)],
            send_sem=grad_send.at[d],
            recv_sem=grad_recv.at[d],
            device_id=(r, lax.rem(s + d, shards)),
            device_id_type=MESH,
        )

    def columns_of(owner, c):
        return features.at[:, pl.ds(pl.multiple_of((owner * chunks + c) * rows, 128), rows)]

    def col_copy(d, c):
        dest = lax.rem(s + d, shards)
        return pltpu.make_async_remote_copy(
            src_ref=columns_of(dest, c),
            dst_ref=cols.at[c, pl.ds(d * tokens, tokens)],
            send_sem=col_send.at[d, c],
            recv_sem=col_recv.at[d, c],
            device_id=(r, dest),
            device_id_type=MESH,
        )

    def loads(c):
        here = pl.ds(pl.multiple_of(c * rows, 16), rows)
        return (
            pltpu.make_async_copy(columns_of(s, c), cols.at[c, pl.ds(0, tokens)], load.at[0, c]),
            pltpu.make_async_copy(moment.at[0, here], mom.at[c], load.at[1, c]),
            pltpu.make_async_copy(error.at[0, here], err.at[c], load.at[2, c]),
        )

    def store_copy(c):
        here = pl.ds(pl.multiple_of(c * rows, 16), rows)
        return pltpu.make_async_copy(mom.at[c], new_worker.at[0, here], store.at[c])

    def pack_copy(c, q):
        owner = c * per + q
        return pltpu.make_async_remote_copy(
            src_ref=packed.at[c, pl.ds(q * owned, owned)],
            dst_ref=got.at[r],
            send_sem=pack_send.at[owner],
            recv_sem=pack_recv.at[r],
            device_id=(owner, s),
            device_id_type=MESH,
        )

    def back_copy(d):
        return pltpu.make_async_remote_copy(
            src_ref=back.at[d],
            dst_ref=input_grads.at[:, pl.ds(pl.multiple_of(s * shard_rows, 128), shard_rows)],
            send_sem=back_send.at[d],
            recv_sem=back_recv.at[d],
            device_id=(r, lax.rem(s + shards - d, shards)),
            device_id_type=MESH,
        )

    def back_arrival(d):
        source = lax.rem(s + d, shards)
        return pltpu.make_async_remote_copy(
            src_ref=back.at[d],
            dst_ref=input_grads.at[:, pl.ds(pl.multiple_of(source * shard_rows, 128), shard_rows)],
            send_sem=back_send.at[d],
            recv_sem=back_recv.at[d],
            device_id=(r, source),
            device_id_type=MESH,
        )

    own_back = pltpu.make_async_copy(
        back.at[0],
        input_grads.at[:, pl.ds(pl.multiple_of(s * shard_rows, 128), shard_rows)],
        back_local,
    )

    def sync_copy(j, place):
        return pltpu.make_async_remote_copy(
            src_ref=block,
            dst_ref=synced.at[pl.ds(pl.multiple_of(place * owned, 16), owned)],
            send_sem=sync_send.at[j],
            recv_sem=sync_recv.at[j],
            device_id=(lax.rem(r + j, replicas), s),
            device_id_type=MESH,
        )

    own_block = pltpu.make_async_copy(
        block, synced.at[pl.ds(pl.multiple_of(r * owned, 16), owned)], sync_local
    )
    load_weight = pltpu.make_async_copy(weight, held_weight, weight_load)
    load_weight.start()
    own_grads = pltpu.make_async_copy(grads, all_grads.at[pl.ds(0, tokens)], grad_local)
    own_grads.start()
    for d in range(1, shards):
        grad_copy(d).start()

    @pl.loop(0, chunks)
    def _(k):
        c = lax.rem(first + k, chunks)
        for d in range(1, shards):
            col_copy(d, c).start()
        for copy in loads(c):
            copy.start()

    own_grads.wait()
    for d in range(1, shards):
        grad_copy(d).wait_recv()
    load_weight.wait()

    @pl.loop(0, chunks)
    def _(c):
        here = pl.ds(pl.multiple_of(c * rows, 128), rows)
        product = lax.dot_general(
            all_grads[...], held_weight[here, :], (((1,), (1,)), ((), ())),
            preferred_element_type=jnp.float32,
        ).astype(jnp.bfloat16)
        for d in range(shards):
            back[d, :, here] = product[d * tokens:(d + 1) * tokens]

    own_back.start()
    for d in range(1, shards):
        back_copy(d).start()

    @pl.loop(0, chunks)
    def _(k):
        c = lax.rem(first + k, chunks)
        for copy in loads(c):
            copy.wait()
        for d in range(1, shards):
            col_copy(d, c).wait_recv()
        grad = lax.dot_general(
            cols[c], all_grads[...], (((0,), (0,)), ((), ())), preferred_element_type=jnp.float32
        )
        value = decay_rate * mom[c] + (1.0 - decay_rate) * grad + err[c]
        small = compress(value)
        mom[c] = value - small.astype(jnp.float32)
        packed[c] = small
        for q in range(per):
            @pl.when(c * per + q != r)
            def _():
                pack_copy(c, q).start()
        store_copy(c).start()

    mine = packed[r // per, pl.ds(pl.multiple_of(lax.rem(r, per) * owned, 16), owned)]
    total[...] = mine.astype(jnp.float32)

    @pl.loop(1, replicas)
    def _(j):
        source = lax.rem(r + j, replicas)
        pltpu.make_async_remote_copy(
            src_ref=packed.at[0, pl.ds(0, owned)],
            dst_ref=got.at[source],
            send_sem=pack_send.at[source],
            recv_sem=pack_recv.at[source],
            device_id=(source, s),
            device_id_type=MESH,
        ).wait_recv()
        total[...] += got[source].astype(jnp.float32)

    held = total[...] / replicas + server[0]
    average = compress(held)
    new_server[0] = held - average.astype(jnp.float32)
    block[...] = average
    own_block.start()

    @pl.loop(1, replicas)
    def _(j):
        sync_copy(j, r).start()

    for d in range(1, shards):
        grad_copy(d).wait_send()

    @pl.loop(0, chunks)
    def _(c):
        for d in range(1, shards):
            col_copy(d, c).wait_send()
        for q in range(per):
            @pl.when(c * per + q != r)
            def _():
                pack_copy(c, q).wait_send()
        store_copy(c).wait()

    own_back.wait()
    own_block.wait()
    for d in range(1, shards):
        back_copy(d).wait_send()
        back_arrival(d).wait_recv()

    @pl.loop(1, replicas)
    def _(j):
        sync_copy(j, r).wait_send()
        sync_copy(j, lax.rem(r + replicas - j, replicas)).wait_recv()


def exchange(features, key_grads, key_weight, momentum, worker_error, server_error):
    shards, replicas = lax.axis_size("shard"), lax.axis_size("replica")
    tokens, width = key_grads.shape
    shard_rows = momentum.shape[1]
    owned = server_error.shape[1]
    rows = owned * max(1, 256 // owned)
    chunks = shard_rows // rows
    any_space = pl.BlockSpec(memory_space=pl.ANY)
    vmem = pl.BlockSpec(memory_space=pltpu.VMEM)
    dma = pltpu.SemaphoreType.DMA
    bf16, f32 = jnp.bfloat16, jnp.float32
    return pl.pallas_call(
        functools.partial(exchange_kernel, shards, replicas),
        in_specs=[any_space] * 5 + [vmem],
        out_specs=[any_space] * 3 + [vmem],
        out_shape=[
            jax.ShapeDtypeStruct(features.shape, bf16),
            jax.ShapeDtypeStruct(key_weight.shape, bf16),
            jax.ShapeDtypeStruct(momentum.shape, f32),
            jax.ShapeDtypeStruct(server_error.shape, f32),
        ],
        scratch_shapes=[
            pltpu.VMEM((owned, width), bf16),
            pltpu.VMEM((shard_rows, width), bf16),
            pltpu.VMEM((shards, tokens, shard_rows), bf16),
            pltpu.VMEM((chunks, shards * tokens, rows), bf16),
            pltpu.VMEM((shards * tokens, width), bf16),
            pltpu.VMEM((chunks, rows, width), f32),
            pltpu.VMEM((chunks, rows, width), f32),
            pltpu.VMEM((chunks, rows, width), bf16),
            pltpu.VMEM((replicas, owned, width), bf16),
            pltpu.VMEM((owned, width), f32),
            dma(()),
            dma((shards,)),
            dma((shards,)),
            dma((3, chunks)),
            dma((shards, chunks)),
            dma((shards, chunks)),
            dma((chunks,)),
            dma((replicas,)),
            dma((replicas,)),
            dma(()),
            dma(()),
            dma((shards,)),
            dma((shards,)),
            dma(()),
            dma((replicas,)),
            dma((replicas,)),
        ],
        compiler_params=pltpu.CompilerParams(
            collective_id=0, has_side_effects=True, vmem_limit_bytes=58 * 2**20
        ),
        cost_estimate=pl.CostEstimate(
            flops=2 * tokens * shards * shard_rows * width,
            bytes_accessed=40 * 2 * tokens * shards * (shard_rows + width),
            transcendentals=shard_rows * width,
        ),
    )(features, key_grads, key_weight, momentum, worker_error, server_error)


def per_device(features, key_grads, key_weight, momentum, worker_error, server_error):
    return tuple(
        exchange(features, key_grads, key_weight, momentum, worker_error, server_error)
    )


def solution(mesh):
    in_specs = (
        P(("replica", "shard"), None),
        P(("replica", "shard"), None),
        P("shard", None),
        P("replica", "shard", None),
        P("replica", "shard", None),
        P("shard", "replica", None),
    )
    out_specs = (
        P(("replica", "shard"), None),
        P("shard", None),
        P("replica", "shard", None),
        P("shard", "replica", None),
    )
    return jax.shard_map(
        per_device, mesh=mesh, in_specs=in_specs, out_specs=out_specs, check_vma=False
    )
```

```python
import functools

import jax
import jax.numpy as jnp
from jax import lax
from jax.experimental import pallas as pl
from jax.experimental.pallas import tpu as pltpu
from jax.sharding import PartitionSpec as P

MESH = pl.DeviceIdType.MESH

decay_rate = 0.9


def compress(values):
    scale = jnp.mean(jnp.abs(values), axis=-1, keepdims=True) + 1e-06
    return (scale * jnp.tanh(values / scale)).astype(jnp.bfloat16)


def exchange_kernel(
    shards, replicas, features, grads, weight, moment, error, server,
    input_grads, synced, new_worker, new_server,
    block, held_weight, back, cols, all_grads, mom, err, packed, got, total,
    grad_local, grad_send, grad_recv, load, col_send, col_recv, store, pack_send, pack_recv,
    weight_load, back_local, far_send, far_recv, plane_send, plane_recv, pair_send, pair_recv, sync_local, sync_send, sync_recv,
):
    r, s = lax.axis_index("replica"), lax.axis_index("shard")
    tokens = grads.shape[0]
    chunks, rows = mom.shape[0], mom.shape[1]
    owned = got.shape[1]
    per = rows // owned
    shard_rows = chunks * rows
    first = r // per + 1

    barrier = pltpu.get_barrier_semaphore()
    for d in range(1, shards):
        pl.semaphore_signal(barrier, inc=1, device_id=(r, lax.rem(s + d, shards)), device_id_type=MESH)
    for d in range(1, replicas):
        pl.semaphore_signal(barrier, inc=1, device_id=(lax.rem(r + d, replicas), s), device_id_type=MESH)
    pl.semaphore_wait(barrier, shards + replicas - 2)

    def grad_copy(d):
        return pltpu.make_async_remote_copy(
            src_ref=grads,
            dst_ref=all_grads.at[pl.ds(d * tokens, tokens)],
            send_sem=grad_send.at[d],
            recv_sem=grad_recv.at[d],
            device_id=(r, lax.rem(s + d, shards)),
            device_id_type=MESH,
        )

    def columns_of(owner, c):
        return features.at[:, pl.ds(pl.multiple_of((owner * chunks + c) * rows, 128), rows)]

    def col_copy(d, c):
        dest = lax.rem(s + d, shards)
        return pltpu.make_async_remote_copy(
            src_ref=columns_of(dest, c),
            dst_ref=cols.at[c, pl.ds(d * tokens, tokens)],
            send_sem=col_send.at[d, c],
            recv_sem=col_recv.at[d, c],
            device_id=(r, dest),
            device_id_type=MESH,
        )

    def loads(c):
        here = pl.ds(pl.multiple_of(c * rows, 16), rows)
        return (
            pltpu.make_async_copy(columns_of(s, c), cols.at[c, pl.ds(0, tokens)], load.at[0, c]),
            pltpu.make_async_copy(moment.at[0, here], mom.at[c], load.at[1, c]),
            pltpu.make_async_copy(error.at[0, here], err.at[c], load.at[2, c]),
        )

    def store_copy(c):
        here = pl.ds(pl.multiple_of(c * rows, 16), rows)
        return pltpu.make_async_copy(mom.at[c], new_worker.at[0, here], store.at[c])

    def pack_copy(c, q):
        owner = c * per + q
        return pltpu.make_async_remote_copy(
            src_ref=packed.at[c, pl.ds(q * owned, owned)],
            dst_ref=got.at[r],
            send_sem=pack_send.at[owner],
            recv_sem=pack_recv.at[r],
            device_id=(owner, s),
            device_id_type=MESH,
        )

    half = replicas // 2
    partner = r + 1 - 2 * lax.rem(r, 2)

    def piece(shard, replica):
        start = shard * shard_rows + replica * owned
        return held_weight.at[pl.ds(pl.multiple_of(start, 16), owned)]

    def far_copy(d):
        return pltpu.make_async_remote_copy(
            src_ref=weight.at[pl.ds(pl.multiple_of(r * owned, 16), owned)],
            dst_ref=piece(s, r),
            send_sem=far_send.at[d],
            recv_sem=far_recv.at[d],
            device_id=(r, lax.rem(s + d, shards)),
            device_id_type=MESH,
        )

    def plane_copy(d, j):
        mine = piece(lax.rem(s + shards - d, shards), r)
        return pltpu.make_async_remote_copy(
            src_ref=mine,
            dst_ref=mine,
            send_sem=plane_send.at[d, j],
            recv_sem=plane_recv.at[d, j],
            device_id=(lax.rem(r + 2 * j, replicas), s),
            device_id_type=MESH,
        )

    def pair_copy(d, j):
        here = piece(lax.rem(s + shards - d, shards), lax.rem(r + replicas - 2 * j, replicas))
        return pltpu.make_async_remote_copy(
            src_ref=here,
            dst_ref=here,
            send_sem=pair_send.at[d, j],
            recv_sem=pair_recv.at[d, j],
            device_id=(partner, s),
            device_id_type=MESH,
        )

    own_back = pltpu.make_async_copy(back, input_grads, back_local)

    def sync_copy(j, place):
        return pltpu.make_async_remote_copy(
            src_ref=block,
            dst_ref=synced.at[pl.ds(pl.multiple_of(place * owned, 16), owned)],
            send_sem=sync_send.at[j],
            recv_sem=sync_recv.at[j],
            device_id=(lax.rem(r + j, replicas), s),
            device_id_type=MESH,
        )

    own_block = pltpu.make_async_copy(
        block, synced.at[pl.ds(pl.multiple_of(r * owned, 16), owned)], sync_local
    )
    load_weight = pltpu.make_async_copy(
        weight, held_weight.at[pl.ds(pl.multiple_of(s * shard_rows, 16), shard_rows)], weight_load
    )
    load_weight.start()
    own_grads = pltpu.make_async_copy(grads, all_grads.at[pl.ds(0, tokens)], grad_local)
    own_grads.start()
    for d in range(1, shards):
        grad_copy(d).start()
    for d in range(1, shards):
        far_copy(d).start()

    @pl.loop(0, chunks)
    def _(k):
        c = lax.rem(first + k, chunks)
        for d in range(1, shards):
            col_copy(d, c).start()
        for copy in loads(c):
            copy.start()

    own_grads.wait()
    for d in range(1, shards):
        grad_copy(d).wait_recv()
    for d in range(1, shards):
        far_copy(d).wait_recv()

        @pl.loop(1, half)
        def _(j):
            plane_copy(d, j).start()

    @pl.loop(0, chunks)
    def _(k):
        c = lax.rem(first + k, chunks)
        for copy in loads(c):
            copy.wait()
        for d in range(1, shards):
            col_copy(d, c).wait_recv()
        grad = lax.dot_general(
            cols[c], all_grads[...], (((0,), (0,)), ((), ())), preferred_element_type=jnp.float32
        )
        value = decay_rate * mom[c] + (1.0 - decay_rate) * grad + err[c]
        small = compress(value)
        mom[c] = value - small.astype(jnp.float32)
        packed[c] = small
        for q in range(per):
            @pl.when(c * per + q != r)
            def _():
                pack_copy(c, q).start()
        store_copy(c).start()

    for d in range(1, shards):
        pair_copy(d, 0).start()

        @pl.loop(1, half)
        def _(j):
            plane_copy(d, j).wait_recv()
            pair_copy(d, j).start()

    mine = packed[r // per, pl.ds(pl.multiple_of(lax.rem(r, per) * owned, 16), owned)]
    total[...] = mine.astype(jnp.float32)

    @pl.loop(1, replicas)
    def _(j):
        source = lax.rem(r + j, replicas)
        pltpu.make_async_remote_copy(
            src_ref=packed.at[0, pl.ds(0, owned)],
            dst_ref=got.at[source],
            send_sem=pack_send.at[source],
            recv_sem=pack_recv.at[source],
            device_id=(source, s),
            device_id_type=MESH,
        ).wait_recv()
        total[...] += got[source].astype(jnp.float32)

    held = total[...] / replicas + server[0]
    average = compress(held)
    new_server[0] = held - average.astype(jnp.float32)
    block[...] = average
    own_block.start()

    @pl.loop(1, replicas)
    def _(j):
        sync_copy(j, r).start()

    load_weight.wait()
    for d in range(1, shards):
        @pl.loop(0, half)
        def _(j):
            pair_copy(d, j).wait_recv()

    @pl.loop(0, shards * chunks)
    def _(i):
        here = pl.ds(pl.multiple_of(i * rows, 128), rows)
        back[:, here] = lax.dot_general(
            all_grads[0:tokens], held_weight[here, :], (((1,), (1,)), ((), ())),
            preferred_element_type=jnp.float32,
        ).astype(jnp.bfloat16)

    own_back.start()

    for d in range(1, shards):
        grad_copy(d).wait_send()

    @pl.loop(0, chunks)
    def _(c):
        for d in range(1, shards):
            col_copy(d, c).wait_send()
        for q in range(per):
            @pl.when(c * per + q != r)
            def _():
                pack_copy(c, q).wait_send()
        store_copy(c).wait()

    own_back.wait()
    own_block.wait()
    for d in range(1, shards):
        far_copy(d).wait_send()

        @pl.loop(1, half)
        def _(j):
            plane_copy(d, j).wait_send()

        @pl.loop(0, half)
        def _(j):
            pair_copy(d, j).wait_send()

    @pl.loop(1, replicas)
    def _(j):
        sync_copy(j, r).wait_send()
        sync_copy(j, lax.rem(r + replicas - j, replicas)).wait_recv()


def exchange(features, key_grads, key_weight, momentum, worker_error, server_error):
    shards, replicas = lax.axis_size("shard"), lax.axis_size("replica")
    tokens, width = key_grads.shape
    shard_rows = momentum.shape[1]
    owned = server_error.shape[1]
    rows = owned * max(1, 256 // owned)
    chunks = shard_rows // rows
    any_space = pl.BlockSpec(memory_space=pl.ANY)
    vmem = pl.BlockSpec(memory_space=pltpu.VMEM)
    dma = pltpu.SemaphoreType.DMA
    bf16, f32 = jnp.bfloat16, jnp.float32
    return pl.pallas_call(
        functools.partial(exchange_kernel, shards, replicas),
        in_specs=[any_space] * 5 + [vmem],
        out_specs=[any_space] * 3 + [vmem],
        out_shape=[
            jax.ShapeDtypeStruct(features.shape, bf16),
            jax.ShapeDtypeStruct(key_weight.shape, bf16),
            jax.ShapeDtypeStruct(momentum.shape, f32),
            jax.ShapeDtypeStruct(server_error.shape, f32),
        ],
        scratch_shapes=[
            pltpu.VMEM((owned, width), bf16),
            pltpu.VMEM((shards * shard_rows, width), bf16),
            pltpu.VMEM((tokens, shards * shard_rows), bf16),
            pltpu.VMEM((chunks, shards * tokens, rows), bf16),
            pltpu.VMEM((shards * tokens, width), bf16),
            pltpu.VMEM((chunks, rows, width), f32),
            pltpu.VMEM((chunks, rows, width), f32),
            pltpu.VMEM((chunks, rows, width), bf16),
            pltpu.VMEM((replicas, owned, width), bf16),
            pltpu.VMEM((owned, width), f32),
            dma(()),
            dma((shards,)),
            dma((shards,)),
            dma((3, chunks)),
            dma((shards, chunks)),
            dma((shards, chunks)),
            dma((chunks,)),
            dma((replicas,)),
            dma((replicas,)),
            dma(()),
            dma(()),
            dma((shards,)),
            dma((shards,)),
            dma((shards, replicas // 2)),
            dma((shards, replicas // 2)),
            dma((shards, replicas // 2)),
            dma((shards, replicas // 2)),
            dma(()),
            dma((replicas,)),
            dma((replicas,)),
        ],
        compiler_params=pltpu.CompilerParams(
            collective_id=0, has_side_effects=True, vmem_limit_bytes=60 * 2**20
        ),
        cost_estimate=pl.CostEstimate(
            flops=2 * tokens * shards * shard_rows * width,
            bytes_accessed=40 * 2 * tokens * shards * (shard_rows + width),
            transcendentals=shard_rows * width,
        ),
    )(features, key_grads, key_weight, momentum, worker_error, server_error)


def per_device(features, key_grads, key_weight, momentum, worker_error, server_error):
    return tuple(
        exchange(features, key_grads, key_weight, momentum, worker_error, server_error)
    )


def solution(mesh):
    in_specs = (
        P(("replica", "shard"), None),
        P(("replica", "shard"), None),
        P("shard", None),
        P("replica", "shard", None),
        P("replica", "shard", None),
        P("shard", "replica", None),
    )
    out_specs = (
        P(("replica", "shard"), None),
        P("shard", None),
        P("replica", "shard", None),
        P("shard", "replica", None),
    )
    return jax.shard_map(
        per_device, mesh=mesh, in_specs=in_specs, out_specs=out_specs, check_vma=False
    )
```
